32 devices in a mesh: gx: 8 (over z, y), gy: 2 (over x), gz: 2 (over core).
Axes of the slice: x: 2, y: 2, z: 4, core: 2. Of those that a mesh axis runs over, the one named last changes fastest.
Arguments:
- pops: float32 [19, 32, 64, 256], P(None, 'gz', 'gx', 'gy'), as said below
- solid: int32 [32, 64, 256], P('gz', 'gx', 'gy'), may hold values 0 or 1
- surf_cell: int32 [2, 8, 2, 512], P('gz', 'gx', 'gy'), may hold values from 0 to 16383
- surf_panel: int32 [2, 8, 2, 512], P('gz', 'gx', 'gy'), may hold values from -1 to 39, as said below
- surf_area: float32 [2, 8, 2, 512], P('gz', 'gx', 'gy'), may hold values from 0.1 to 1
- mode_shape: float32 [2, 8, 2, 12, 512], P('gz', 'gx', 'gy'), may hold values from -5 to 5
- mode_of_panel: int32 [40], replicated, may hold values from 0 to 11
- compliance: float32 [12], replicated, may hold values from 0.3 to 3
Outputs:
- read: float32 [19, 32, 64, 256], P(None, 'gz', 'gx', 'gy')
- panel_force: float32 [40], replicated
- mode_amplitude: float32 [12], replicated
The draws below stay inside these ranges and needn't reach their ends.
Inputs may be any that keep to these rules, and one draw needn't show every extreme that they name: pops is positive, with densities near 1 and flow speeds below 0.25. `surf_panel`: -1 marks an empty slot; on each device the live slots come first, at least 64 of them; some device has all 512 slots live; one panel's surfels lie on at most about 40 consecutive bricks in the linear order (vertical, streamwise, crosswise) of the devices, counted periodically so that the last brick is followed by the first.
All inputs are finite; a program needn't handle non-finite values. No bound on the sum of `solid` on one device may be relied on, other than what follows from the above.
Results may differ from the reference program's by a relative error of at most 0.00011.
Values sent between devices are 32-bit elements; how exact they have to be, the bound alone decides.
A program may use at most 64 MiB of HBM per device.

```python
import math
import jax
import jax.numpy as jnp

PANELS = 40
MODES = 12
CZ = 16
CX = 8
CY = 128
S_DEV = 512
NZ = 32
NX = 64
NY = 256
N_GX = 8
N_GY = 2
N_GZ = 2


VELOCITY = ((0, 0, 0), (1, 0, 0), (-1, 0, 0), (0, 1, 0), (0, -1, 0), (0, 0, 1), (0, 0, -1), (1, 1, 0), (-1, -1, 0), (1, -1, 0), (-1, 1, 0), (1, 0, 1), (-1, 0, -1), (1, 0, -1), (-1, 0, 1), (0, 1, 1), (0, -1, -1), (0, 1, -1), (0, -1, 1))


WEIGHTS = (1.0 / 3.0,) + (1.0 / 18.0,) * 6 + (1.0 / 36.0,) * 12


def draw_pops(key, part):
    shape3 = (NZ, NX, NY)
    keys = jax.random.split(key, 5)
    density = 1.0 + 0.05 * jax.random.truncated_normal(keys[0], -4.0, 4.0, shape3, jnp.float32)
    flows = [0.04 * jax.random.truncated_normal(keys[1 + axis], -4.0, 4.0, shape3, jnp.float32) for axis in range(3)]
    squared = flows[0] * flows[0] + flows[1] * flows[1] + flows[2] * flows[2]
    noise = jax.random.truncated_normal(keys[4], -4.0, 4.0, (19,) + shape3, jnp.float32)
    result = []
    for index in range(19):
        vel = VELOCITY[index]
        projected = vel[0] * flows[0] + vel[1] * flows[1] + vel[2] * flows[2]
        equilib = WEIGHTS[index] * density * (1.0 + 3.0 * projected + 4.5 * projected * projected - 1.5 * squared)
        result.append(equilib + 0.005 * WEIGHTS[index] * noise[index])
    return jnp.stack(result).astype(jnp.float32)


def draw_surf_panel(key, part):
    ndev = N_GZ * N_GX * N_GY
    linear = jnp.arange(ndev, dtype=jnp.int32).reshape(N_GZ, N_GX, N_GY, 1)
    first, second = jax.random.split(key, 2)
    base = linear * PANELS // ndev
    offset = jax.random.randint(first, (N_GZ, N_GX, N_GY, S_DEV), 0, 3, jnp.int32)
    slot = jnp.arange(S_DEV, dtype=jnp.int32)
    offset = jnp.where(slot == 0, 0, offset)
    panel = (base + offset) % PANELS
    live_count = jax.random.randint(second, (N_GZ, N_GX, N_GY, 1), S_DEV // 8, S_DEV + 1, jnp.int32)
    live_count = jnp.where(linear == 0, S_DEV, live_count)
    live_count = jnp.where(linear == ndev - 1, S_DEV // 8, live_count)
    return jnp.where(slot < live_count, panel, -1).astype(jnp.int32)


def plant(entries, rng, smallest, largest):
    extent = entries.shape
    place = [jax.random.randint(jax.random.fold_in(rng, axis), (), 0, extent[axis]) for axis in range(len(extent))]
    entries = entries.at[tuple(place)].set(smallest)
    longest = extent.index(max(extent))
    place[longest] = (place[longest] + 1) % extent[longest]
    return entries.at[tuple(place)].set(largest)


def level_of(stream_key, shape, pieces, least, high):
    factor_of, own = 1.0, jax.random.fold_in(stream_key, 6)
    for dim, parts in pieces:
        heights = jnp.exp(jax.random.uniform(jax.random.fold_in(own, dim), (parts,), jnp.float32, least / len(pieces), high / len(pieces)))
        factor_of = factor_of * jnp.repeat(heights, shape[dim] // parts).reshape([-1 if axis == dim else 1 for axis in range(len(shape))])
    return factor_of


def bell_draw(stream_key, dims, width, limit, cuts=(), kind=jnp.bfloat16):
    values = jax.random.normal(stream_key, dims, jnp.float32) * width
    if len(cuts) > 0:
        values = level_of(stream_key, dims, cuts, -0.22, 0.18) * values
    return jnp.clip(values, min=-limit, max=limit).astype(kind)


def setup_inputs(seed: int = 0) -> dict:
    seeds = jax.random.split(jax.random.key(seed), 9)
    pops = draw_pops(jax.random.fold_in(seeds[8], 71), 0)
    solid = plant((jax.random.randint(seeds[1], (NZ, NX, NY), 0, 8) < 1).astype(jnp.int32), jax.random.fold_in(seeds[1], 1), 0, 1)
    surf_cell = plant(jax.random.randint(seeds[2], (N_GZ, N_GX, N_GY, S_DEV), 0, CZ * CX * CY), jax.random.fold_in(seeds[2], 1), 0, (CZ * CX * CY) - 1).astype(jnp.int32)
    surf_panel = draw_surf_panel(jax.random.fold_in(seeds[8], 71), 0)
    surf_area = jnp.clip(jnp.exp(math.log(1.0) - 2.3025851 * jax.random.uniform(seeds[4], (N_GZ, N_GX, N_GY, S_DEV), jnp.float32) ** level_of(seeds[4], (N_GZ, N_GX, N_GY, S_DEV), ((0, 2), (1, 8), (2, 2)), -0.2, 0.2)), 0.1, 1.0)
    mode_shape = bell_draw(seeds[5], (N_GZ, N_GX, N_GY, MODES, S_DEV), 1.0, 5.0, ((0, 2), (1, 8), (2, 2)), jnp.float32)
    mode_of_panel = plant(jax.random.randint(seeds[6], (PANELS,), 0, MODES), jax.random.fold_in(seeds[6], 1), 0, MODES - 1).astype(jnp.int32)
    compliance = jnp.clip(jnp.exp(jax.random.uniform(seeds[7], (MODES,), jnp.float32, math.log(0.3), math.log(3.0))), 0.3, 3.0)
    return {"pops": pops, "solid": solid, "surf_cell": surf_cell, "surf_panel": surf_panel, "surf_area": surf_area, "mode_shape": mode_shape, "mode_of_panel": mode_of_panel, "compliance": compliance}


VELOCITY = ((0, 0, 0), (1, 0, 0), (-1, 0, 0), (0, 1, 0), (0, -1, 0), (0, 0, 1), (0, 0, -1),
            (1, 1, 0), (-1, -1, 0), (1, -1, 0), (-1, 1, 0), (1, 0, 1), (-1, 0, -1),
            (1, 0, -1), (-1, 0, 1), (0, 1, 1), (0, -1, -1), (0, 1, -1), (0, -1, 1))
WEIGHTS = (1.0 / 3.0,) + (1.0 / 18.0,) * 6 + (1.0 / 36.0,) * 12
OPPOSITE = (0, 2, 1, 4, 3, 6, 5, 8, 7, 10, 9, 12, 11, 14, 13, 16, 15, 18, 17)
OMEGA = 1.0 / 0.6
WALL_SCALE = 0.02


def collide(pops, solid):
    density = pops[0]
    for index in range(1, 19):
        density = density + pops[index]
    moments = []
    for axis in range(3):
        total = jnp.zeros_like(density)
        for index in range(19):
            comp = VELOCITY[index][axis]
            if comp == 1:
                total = total + pops[index]
            elif comp == -1:
                total = total - pops[index]
        moments.append(total / density)
    squared = moments[0] * moments[0] + moments[1] * moments[1] + moments[2] * moments[2]
    result = []
    for index in range(19):
        projected = jnp.zeros_like(density)
        for axis in range(3):
            comp = VELOCITY[index][axis]
            if comp == 1:
                projected = projected + moments[axis]
            elif comp == -1:
                projected = projected - moments[axis]
        equilib = WEIGHTS[index] * density * (1.0 + 3.0 * projected + 4.5 * projected * projected - 1.5 * squared)
        relaxed = pops[index] + OMEGA * (equilib - pops[index])
        result.append(jnp.where(solid == 1, pops[OPPOSITE[index]], relaxed))
    return density, result


def reference(pops, solid, surf_cell, surf_panel, surf_area, mode_shape, mode_of_panel, compliance):
    density, post = collide(pops, solid)
    ndev = N_GZ * N_GX * N_GY
    cells = CZ * CX * CY
    bricks = density.reshape(N_GZ, CZ, N_GX, CX, N_GY, CY).transpose(0, 2, 4, 1, 3, 5).reshape(ndev, cells)
    cell_rows = surf_cell.reshape(ndev, S_DEV)
    panel_rows = surf_panel.reshape(ndev, S_DEV)
    gathered = jnp.take_along_axis(bricks, cell_rows, axis=1)
    live = panel_rows >= 0
    contrib = jnp.where(live, surf_area.reshape(ndev, S_DEV) * ((gathered - 1.0) / 3.0), 0.0)
    panel_ids = jnp.arange(PANELS, dtype=jnp.int32)
    panel_force = jnp.sum(jnp.where(panel_rows[:, :, None] == panel_ids, contrib[:, :, None], 0.0), axis=(0, 1))
    mode_ids = jnp.arange(MODES, dtype=jnp.int32)
    mode_load = jnp.sum(jnp.where(mode_of_panel[:, None] == mode_ids[None, :], panel_force[:, None], 0.0), axis=0)
    mode_amplitude = compliance * mode_load
    shapes = mode_shape.reshape(ndev, MODES, S_DEV)
    wall = WALL_SCALE * jnp.sum(mode_amplitude[None, :, None] * shapes, axis=1)
    values = jnp.where(live, gathered * wall, 0.0)
    rows = jnp.arange(ndev, dtype=jnp.int32)[:, None]
    flux_bricks = jnp.zeros((ndev, cells), jnp.float32).at[rows, cell_rows].add(values)
    wall_flux = flux_bricks.reshape(N_GZ, N_GX, N_GY, CZ, CX, CY).transpose(0, 3, 1, 4, 2, 5).reshape(NZ, NX, NY)
    read = []
    for index in range(19):
        coef = 6.0 * WEIGHTS[index] * VELOCITY[index][0]
        corrected = post[index] + coef * wall_flux
        vel = VELOCITY[index]
        read.append(jnp.roll(corrected, (vel[2], vel[0], vel[1]), axis=(0, 1, 2)))
    return jnp.stack(read), panel_force, mode_amplitude
```

```python
import functools

import jax
import jax.numpy as jnp
from jax import lax
from jax.experimental import pallas as pl
from jax.experimental.pallas import tpu as pltpu
from jax.sharding import PartitionSpec as P

PANELS = 40
MODES = 12
VELOCITY = (
    (0, 0, 0),
    (1, 0, 0),
    (-1, 0, 0),
    (0, 1, 0),
    (0, -1, 0),
    (0, 0, 1),
    (0, 0, -1),
    (1, 1, 0),
    (-1, -1, 0),
    (1, -1, 0),
    (-1, 1, 0),
    (1, 0, 1),
    (-1, 0, -1),
    (1, 0, -1),
    (-1, 0, 1),
    (0, 1, 1),
    (0, -1, -1),
    (0, 1, -1),
    (0, -1, 1),
)
WEIGHTS = (1.0 / 3.0,) + (1.0 / 18.0,) * 6 + (1.0 / 36.0,) * 12
OMEGA = 1.0 / 0.6
WALL_SCALE = 0.02
COEF = tuple(6.0 * w * v[0] for w, v in zip(WEIGHTS, VELOCITY))
SIGNS = (1, -1)


def moving(axis, sign):
    return tuple(i for i in range(19) if VELOCITY[i][axis] == sign)


X_GROUP = tuple(moving(0, s) for s in SIGNS)
Y_GROUP = tuple(moving(1, s) for s in SIGNS)
Z_GROUP = tuple(moving(2, s) for s in SIGNS)
ORDER = Z_GROUP[0] + Z_GROUP[1] + tuple(i for i in range(19) if VELOCITY[i][2] == 0)
PLACE = tuple(ORDER.index(i) for i in range(19))
AXES = ("gx", "gy", "gz")
STAGES = (("gx",), ("gy", "gz"))
MESH = pl.DeviceIdType.MESH
F32 = jnp.float32
BF16 = jnp.bfloat16


def halves(x):
    high = x.astype(BF16)
    return high, (x - high.astype(F32)).astype(BF16)


def dot(a, b):
    return jnp.dot(a, b, preferred_element_type=F32)


def dot_nt(a, b):
    return lax.dot_general(a, b, (((1,), (1,)), ((), ())), preferred_element_type=F32)


def shift_of(velocity):
    return (velocity[0], velocity[1], velocity[2])


def offsets_of(sizes):
    found = []
    for i in range(1, 19):
        found.append(tuple(c % n for c, n in zip(VELOCITY[i], sizes)))
    for stage in STAGES:
        for offset in stage_offsets(stage, sizes):
            found.append(offset)
    return sorted(set(found))


def stage_offsets(stage, sizes):
    result = [(0, 0, 0)]
    for dim, axis in enumerate(AXES):
        if axis in stage:
            result = [
                tuple(k if d == dim else o[d] for d in range(3))
                for o in result
                for k in range(sizes[dim])
            ]
    return [o for o in result if o != (0, 0, 0)]


def kernel(
    sizes,
    pops,
    solid,
    cell,
    panel,
    area,
    shapes,
    panel_mode,
    compliance,
    out,
    force_out,
    amp_out,
    post,
    dens,
    wall,
    xs,
    xh,
    wxs,
    wxh,
    ys,
    yh,
    yxh,
    yzh,
    ws,
    wh,
    wyx,
    slots_a,
    slots_b,
    send_sem,
    recv_sem,
    send_a,
    recv_a,
    send_b,
    recv_b,
):
    depth, rows, width = pops.shape[1:]
    cells = depth * rows
    here = tuple(lax.axis_index(a) for a in AXES)

    def at(offset):
        return tuple(lax.rem(h + o % n, n) if o % n else h for h, o, n in zip(here, offset, sizes))

    partners = offsets_of(sizes)
    barrier = pltpu.get_barrier_semaphore()
    for offset in partners:
        pl.semaphore_signal(barrier, inc=1, device_id=at(offset), device_id_type=MESH)

    lane = lax.broadcasted_iota(jnp.int32, (rows, width), 1)
    sub = lax.broadcasted_iota(jnp.int32, (rows, width), 0)

    def collide(z, packed):
        f = [pops[i, z] for i in range(19)]
        density = f[0]
        for i in range(1, 19):
            density = density + f[i]
        inverse = 1.0 / density
        u = []
        for axis in range(3):
            plus, minus = moving(axis, 1), moving(axis, -1)
            total = f[plus[0]] - f[minus[0]]
            for i, j in zip(plus[1:], minus[1:]):
                total = total + (f[i] - f[j])
            u.append(total * inverse)
        base = 1.0 - 1.5 * (u[0] * u[0] + u[1] * u[1] + u[2] * u[2])
        fixed = solid[z] == 1
        dens[z] = density
        scaled = [OMEGA * w * density for w in WEIGHTS]
        new = [None] * 19
        new[0] = jnp.where(fixed, f[0], (1.0 - OMEGA) * f[0] + scaled[0] * base)
        for i in range(1, 19, 2):
            proj = None
            for axis in range(3):
                comp = VELOCITY[i][axis]
                if comp:
                    term = u[axis] if comp == 1 else -u[axis]
                    proj = term if proj is None else proj + term
            even = scaled[i] * (base + 4.5 * (proj * proj))
            odd = scaled[i] * (3.0 * proj)
            new[i] = jnp.where(fixed, f[i + 1], (1.0 - OMEGA) * f[i] + (even + odd))
            new[i + 1] = jnp.where(fixed, f[i], (1.0 - OMEGA) * f[i + 1] + (even - odd))
        for i in range(19):
            post[PLACE[i], z + 1] = new[i]
        packed = list(packed)
        for a in range(2):
            edge = rows - 1 if a == 0 else 0
            for k, i in enumerate(X_GROUP[a]):
                xs[a, k, z] = new[i][edge : edge + 1]
            edge = width - 1 if a == 0 else 0
            for j, i in enumerate(Y_GROUP[a]):
                column = jnp.broadcast_to(new[i][:, edge : edge + 1], (rows, width))
                packed[a] = jnp.where(lane == j * depth + z, column, packed[a])
        return tuple(packed)

    zero = jnp.zeros((rows, width), F32)
    packed = lax.fori_loop(0, depth, collide, (zero, zero))
    for a in range(2):
        ys[a] = packed[a]

    live = panel[...] >= 0
    col = lax.rem(cell[...], width)
    row = lax.div(cell[...], width)
    n_surf = cell.shape[1]
    pick_col = jnp.where(
        lax.broadcasted_iota(jnp.int32, (width, n_surf), 0) == col, 1.0, 0.0
    ).astype(BF16)
    on_row = lax.broadcasted_iota(jnp.int32, (cells, n_surf), 0) == row
    gauge_high, gauge_low = halves(dens[...].reshape(cells, width) - 1.0)
    by_row = dot(gauge_high, pick_col) + dot(gauge_low, pick_col)
    excess = jnp.sum(jnp.where(on_row, by_row, 0.0), axis=0, keepdims=True)
    contrib = jnp.where(live, area[...] * (excess / 3.0), 0.0)
    pick_panel = jnp.where(
        lax.broadcasted_iota(jnp.int32, (width, n_surf), 0) == panel[...], 1.0, 0.0
    ).astype(BF16)
    contrib_high, contrib_low = halves(jnp.broadcast_to(contrib, (8, n_surf)))
    partial = dot_nt(contrib_high, pick_panel) + dot_nt(contrib_low, pick_panel)
    partial = partial[0:1]

    pl.semaphore_wait(barrier, len(partners))

    def stage_start(stage, slots, send, recv, value):
        index = 0
        for dim, axis in enumerate(AXES):
            if axis in stage:
                index = index * sizes[dim] + here[dim]
        slots[index] = value
        copies = []
        for n, offset in enumerate(stage_offsets(stage, sizes)):
            copy = pltpu.make_async_remote_copy(
                src_ref=slots.at[index],
                dst_ref=slots.at[index],
                send_sem=send.at[n],
                recv_sem=recv.at[n],
                device_id=at(offset),
                device_id_type=MESH,
            )
            copy.start()
            copies.append(copy)
        return copies

    def stage_sum(slots, copies):
        for copy in copies:
            copy.wait()
        total = slots[0]
        for n in range(1, slots.shape[0]):
            total = total + slots[n]
        return total

    copies_a = stage_start(STAGES[0], slots_a, send_a, recv_a, partial)

    halo = []

    def send(src, dst, offset):
        copy = pltpu.make_async_remote_copy(
            src_ref=src,
            dst_ref=dst,
            send_sem=send_sem.at[len(halo)],
            recv_sem=recv_sem.at[len(halo)],
            device_id=at(offset),
            device_id_type=MESH,
        )
        copy.start()
        halo.append(copy)
        return copy

    for a, s in enumerate(SIGNS):
        group = Z_GROUP[a]
        first = a * len(group)
        source, target = (depth, 0) if a == 0 else (1, depth + 1)
        send(xs.at[a], xh.at[a, :, pl.ds(1, depth)], (s, 0, 0))
        send(
            post.at[pl.ds(first, len(group)), source],
            post.at[pl.ds(first, len(group)), target],
            (0, 0, s),
        )
        send(ys.at[a], yh.at[a], (0, s, 0))
        for b, t in enumerate(SIGNS):
            send(ys.at[a], yxh.at[a, b], (t, s, 0))
            send(ys.at[a], yzh.at[a, b], (0, s, t))
            k = [i for i in range(5) if VELOCITY[X_GROUP[a][i]][2] == t][0]
            source, target = (depth - 1, 0) if b == 0 else (0, depth + 1)
            send(xs.at[a, k, source], xh.at[a, k, target], (s, 0, t))

    mode_id = lax.broadcasted_iota(jnp.int32, (MODES, PANELS), 0)
    diagonal = lax.broadcasted_iota(jnp.int32, (MODES, MODES), 0) == lax.broadcasted_iota(
        jnp.int32, (MODES, MODES), 1
    )
    factor = jnp.sum(jnp.where(diagonal, compliance[...], 0.0), axis=1, keepdims=True)
    drives = panel_mode[...] == mode_id

    load_a = stage_sum(slots_a, copies_a)
    copies_b = stage_start(STAGES[1], slots_b, send_b, recv_b, load_a)
    force = stage_sum(slots_b, copies_b)[:, :PANELS]
    force_out[...] = force
    amp = factor * jnp.sum(jnp.where(drives, force, 0.0), axis=1, keepdims=True)
    amp_out[...] = jnp.sum(jnp.where(diagonal, amp, 0.0), axis=0, keepdims=True)

    speed = WALL_SCALE * jnp.sum(amp * shapes[...], axis=0, keepdims=True)
    speed = jnp.where(live, speed, 0.0)
    high, low = halves(jnp.where(on_row, speed, 0.0))
    flux = dot_nt(high, pick_col) + dot_nt(low, pick_col)
    flux = flux.reshape(depth, rows, width) * dens[...]
    wall[pl.ds(1, depth)] = flux

    def pack_wall(z, packed):
        value = wall[z + 1]
        packed = list(packed)
        for a in range(2):
            edge = rows - 1 if a == 0 else 0
            wxs[a, z] = value[edge : edge + 1]
            edge = width - 1 if a == 0 else 0
            column = jnp.broadcast_to(value[:, edge : edge + 1], (rows, width))
            for j, i in enumerate(Y_GROUP[a]):
                if VELOCITY[i][0]:
                    packed[a] = jnp.where(lane == j * depth + z, COEF[i] * column, packed[a])
        return tuple(packed)

    packed = lax.fori_loop(0, depth, pack_wall, (zero, zero))
    n_post = len(halo)
    for a, s in enumerate(SIGNS):
        ws[a] = packed[a]
        source, target = (depth, 0) if a == 0 else (1, depth + 1)
        send(wxs.at[a], wxh.at[a, pl.ds(1, depth)], (s, 0, 0))
        send(wall.at[source], wall.at[target], (0, 0, s))
        send(ws.at[a], wh.at[a], (0, s, 0))
        for b, t in enumerate(SIGNS):
            send(ws.at[a], wyx.at[a, b], (t, s, 0))
            source, target = (depth - 1, 0) if b == 0 else (0, depth + 1)
            send(wxs.at[a, source], wxh.at[a, target], (s, 0, t))

    for copy in halo:
        copy.wait()

    columns = []
    for a in range(2):
        face = yh[a] + wh[a]
        result = face
        for j, i in enumerate(Y_GROUP[a]):
            cx, _, cz = VELOCITY[i]
            mine = (lane >= j * depth) & (lane < (j + 1) * depth)
            if cx:
                b = SIGNS.index(cx)
                edge = yxh[a, b] + wyx[a, b]
                whole = pltpu.roll(face, cx % rows, 0)
                whole = jnp.where(sub == (0 if cx == 1 else rows - 1), pltpu.roll(edge, cx % rows, 0), whole)
                result = jnp.where(mine, whole, result)
            if cz:
                b = SIGNS.index(cz)
                whole = pltpu.roll(face, cz % width, 1)
                wrapped = pltpu.roll(yzh[a, b], (-cz * (depth - 1)) % width, 1)
                spot = j * depth if cz == 1 else (j + 1) * depth - 1
                result = jnp.where(mine, jnp.where(lane == spot, wrapped, whole), result)
        columns.append(result)

    def finish(z, columns):
        for i in range(19):
            cx, cy, cz = VELOCITY[i]
            source = z + 1 - cz
            value = post[PLACE[i], source]
            if cx:
                a = SIGNS.index(cx)
                k = X_GROUP[a].index(i)
                value = value + COEF[i] * wall[source]
                line = xh[a, k, source] + COEF[i] * wxh[a, source]
                value = pltpu.roll(value, cx % rows, 0)
                value = jnp.where(sub == (0 if cx == 1 else rows - 1), line, value)
            if cy:
                a = SIGNS.index(cy)
                j = Y_GROUP[a].index(i)
                value = pltpu.roll(value, cy % width, 1)
                column = jnp.broadcast_to(
                    columns[a][:, j * depth : j * depth + 1], (rows, width)
                )
                value = jnp.where(lane == (0 if cy == 1 else width - 1), column, value)
            out[i, z] = value
        return tuple(pltpu.roll(c, width - 1, 1) for c in columns)

    lax.fori_loop(0, depth, finish, tuple(columns))


def per_device(sizes, pops, solid, cell, panel, area, shapes, panel_mode, compliance):
    depth, rows, width = pops.shape[1:]
    n_surf = cell.shape[-1]
    count = {a: n for a, n in zip(AXES, sizes)}
    n_a, n_b = (
        functools.reduce(lambda x, y: x * y, [count[a] for a in stage]) for stage in STAGES
    )
    vmem = pl.BlockSpec(memory_space=pltpu.VMEM)
    tile = (rows, width)
    messages = 18 + 14
    dma = pltpu.SemaphoreType.DMA
    read, force, amp = pl.pallas_call(
        functools.partial(kernel, sizes),
        out_shape=(
            jax.ShapeDtypeStruct(pops.shape, F32),
            jax.ShapeDtypeStruct((1, PANELS), F32),
            jax.ShapeDtypeStruct((1, MODES), F32),
        ),
        in_specs=[vmem] * 8,
        out_specs=(vmem,) * 3,
        scratch_shapes=[
            pltpu.VMEM((19, depth + 2) + tile, F32),
            pltpu.VMEM((depth,) + tile, F32),
            pltpu.VMEM((depth + 2,) + tile, F32),
            pltpu.VMEM((2, 5, depth, 1, width), F32),
            pltpu.VMEM((2, 5, depth + 2, 1, width), F32),
            pltpu.VMEM((2, depth, 1, width), F32),
            pltpu.VMEM((2, depth + 2, 1, width), F32),
            pltpu.VMEM((2,) + tile, F32),
            pltpu.VMEM((2,) + tile, F32),
            pltpu.VMEM((2, 2) + tile, F32),
            pltpu.VMEM((2, 2) + tile, F32),
            pltpu.VMEM((2,) + tile, F32),
            pltpu.VMEM((2,) + tile, F32),
            pltpu.VMEM((2, 2) + tile, F32),
            pltpu.VMEM((n_a, 1, width), F32),
            pltpu.VMEM((n_b, 1, width), F32),
            dma((messages,)),
            dma((messages,)),
            dma((n_a - 1,)),
            dma((n_a - 1,)),
            dma((n_b - 1,)),
            dma((n_b - 1,)),
        ],
        compiler_params=pltpu.CompilerParams(
            collective_id=0, has_side_effects=True, vmem_limit_bytes=32 * 1024 * 1024
        ),
    )(
        pops,
        solid,
        cell.reshape(1, n_surf),
        panel.reshape(1, n_surf),
        area.reshape(1, n_surf),
        shapes.reshape(MODES, n_surf),
        panel_mode.reshape(1, PANELS),
        compliance.reshape(1, MODES),
    )
    return read, force.reshape(PANELS), amp.reshape(MODES)


def solution(mesh):
    placed = (
        P(None, "gz", "gx", "gy"),
        P("gz", "gx", "gy"),
        P("gz", "gx", "gy", None),
        P("gz", "gx", "gy", None),
        P("gz", "gx", "gy", None),
        P("gz", "gx", "gy", None, None),
        P(),
        P(),
    )
    return jax.shard_map(
        functools.partial(per_device, tuple(mesh.shape[a] for a in AXES)),
        mesh=mesh,
        in_specs=placed,
        out_specs=(P(None, "gz", "gx", "gy"), P(), P()),
        check_vma=False,
    )
```

```python
import functools

import jax
import jax.numpy as jnp
from jax import lax
from jax.experimental import pallas as pl
from jax.experimental.pallas import tpu as pltpu
from jax.sharding import PartitionSpec as P

PANELS = 40
MODES = 12
VELOCITY = (
    (0, 0, 0),
    (1, 0, 0),
    (-1, 0, 0),
    (0, 1, 0),
    (0, -1, 0),
    (0, 0, 1),
    (0, 0, -1),
    (1, 1, 0),
    (-1, -1, 0),
    (1, -1, 0),
    (-1, 1, 0),
    (1, 0, 1),
    (-1, 0, -1),
    (1, 0, -1),
    (-1, 0, 1),
    (0, 1, 1),
    (0, -1, -1),
    (0, 1, -1),
    (0, -1, 1),
)
WEIGHTS = (1.0 / 3.0,) + (1.0 / 18.0,) * 6 + (1.0 / 36.0,) * 12
OMEGA = 1.0 / 0.6
WALL_SCALE = 0.02
COEF = tuple(6.0 * w * v[0] for w, v in zip(WEIGHTS, VELOCITY))
SIGNS = (1, -1)


def moving(axis, sign):
    return tuple(i for i in range(19) if VELOCITY[i][axis] == sign)


X_GROUP = tuple(moving(0, s) for s in SIGNS)
Y_GROUP = tuple(moving(1, s) for s in SIGNS)
Z_GROUP = tuple(moving(2, s) for s in SIGNS)
ORDER = Z_GROUP[0] + Z_GROUP[1] + tuple(i for i in range(19) if VELOCITY[i][2] == 0)
PLACE = tuple(ORDER.index(i) for i in range(19))
AXES = ("gx", "gy", "gz")
STAGES = (("gx",), ("gy", "gz"))
MESH = pl.DeviceIdType.MESH
N_LOADS = 4
F32 = jnp.float32
BF16 = jnp.bfloat16


def halves(x):
    high = x.astype(BF16)
    return high, (x - high.astype(F32)).astype(BF16)


def dot(a, b):
    return jnp.dot(a, b, preferred_element_type=F32)


def dot_nt(a, b):
    return lax.dot_general(a, b, (((1,), (1,)), ((), ())), preferred_element_type=F32)


def shift_of(velocity):
    return (velocity[0], velocity[1], velocity[2])


def offsets_of(sizes):
    found = []
    for i in range(1, 19):
        found.append(tuple(c % n for c, n in zip(VELOCITY[i], sizes)))
    for stage in STAGES:
        for offset in stage_offsets(stage, sizes):
            found.append(offset)
    return sorted(set(found))


def stage_offsets(stage, sizes):
    result = [(0, 0, 0)]
    for dim, axis in enumerate(AXES):
        if axis in stage:
            result = [
                tuple(k if d == dim else o[d] for d in range(3))
                for o in result
                for k in range(sizes[dim])
            ]
    return [o for o in result if o != (0, 0, 0)]


WALLS = []
for first, s in enumerate(SIGNS):
    WALLS.append(("x", first, 0, (s, 0, 0)))
    WALLS.append(("y", first, 0, (0, s, 0)))
    WALLS.append(("z", first, 0, (0, 0, s)))
    for second, t in enumerate(SIGNS):
        WALLS.append(("xz", first, second, (s, 0, t)))
        WALLS.append(("yx", first, second, (t, s, 0)))


def wall_offsets(sizes):
    return sorted({tuple(c % n for c, n in zip(w[3], sizes)) for w in WALLS})


def kernel(
    sizes,
    pops_in,
    solid_in,
    cell_in,
    panel_in,
    area_in,
    shapes_in,
    panel_mode_in,
    compliance_in,
    out,
    force_out,
    amp_out,
    pops,
    solid,
    cell,
    panel,
    area,
    shape_rows,
    panel_mode,
    compliance,
    mine,
    load_sem,
    post,
    dens,
    wall,
    xs,
    xh,
    wxh,
    ys,
    yh,
    yxh,
    yzh,
    theirs,
    picks,
    surf_send,
    surf_recv,
    slots_a,
    slots_b,
    send_sem,
    recv_sem,
    send_a,
    recv_a,
    send_b,
    recv_b,
):
    depth, rows, width = pops.shape[1:]
    cells = depth * rows
    here = tuple(lax.axis_index(a) for a in AXES)

    def at(offset):
        return tuple(lax.rem(h + o % n, n) if o % n else h for h, o, n in zip(here, offset, sizes))

    partners = offsets_of(sizes)
    barrier = pltpu.get_barrier_semaphore()
    for offset in partners:
        pl.semaphore_signal(barrier, inc=1, device_id=at(offset), device_id_type=MESH)

    pairs = [(cell_in, cell), (panel_in, panel), (area_in, area)]
    pairs += [(solid_in, solid), (shapes_in, shape_rows)]
    pairs += [(panel_mode_in, panel_mode), (compliance_in, compliance)]
    part = depth // N_LOADS
    cuts = [pl.ds(n * part, part) for n in range(N_LOADS)]
    pairs = pairs[:3] + [(pops_in.at[:, c], pops.at[:, c]) for c in cuts] + pairs[3:]
    loads = []
    for n, (src, dst) in enumerate(pairs):
        loads.append(pltpu.make_async_copy(src, dst, load_sem.at[n]))
        loads[n].start()

    lane = lax.broadcasted_iota(jnp.int32, (rows, width), 1)
    sub = lax.broadcasted_iota(jnp.int32, (rows, width), 0)

    for copy in loads[:3]:
        copy.wait()
    live = panel[...] >= 0
    col = lax.rem(cell[...], width)
    row = lax.div(cell[...], width)
    n_surf = cell.shape[1]
    pick_col = jnp.where(
        lax.broadcasted_iota(jnp.int32, (width, n_surf), 0) == col, 1.0, 0.0
    ).astype(BF16)
    on_row = lax.broadcasted_iota(jnp.int32, (cells, n_surf), 0) == row

    def add_up(z, carry):
        density = pops[0, z]
        for i in range(1, 19):
            density = density + pops[i, z]
        dens[z + 1] = density
        return carry

    for n in range(N_LOADS):
        loads[3 + n].wait()
        lax.fori_loop(n * part, (n + 1) * part, add_up, 0)
    gauge_high, gauge_low = halves(dens[pl.ds(1, depth)].reshape(cells, width) - 1.0)
    by_row = dot(gauge_high, pick_col) + dot(gauge_low, pick_col)
    excess = jnp.sum(jnp.where(on_row, by_row, 0.0), axis=0, keepdims=True)
    contrib = jnp.where(live, area[...] * (excess / 3.0), 0.0)
    pick_panel = jnp.where(
        lax.broadcasted_iota(jnp.int32, (width, n_surf), 0) == panel[...], 1.0, 0.0
    ).astype(BF16)
    contrib_high, contrib_low = halves(jnp.broadcast_to(contrib, (8, n_surf)))
    partial = dot_nt(contrib_high, pick_panel) + dot_nt(contrib_low, pick_panel)
    partial = partial[0:1]

    pl.semaphore_wait(barrier, len(partners))

    def stage_start(stage, slots, send, recv, value):
        index = 0
        for dim, axis in enumerate(AXES):
            if axis in stage:
                index = index * sizes[dim] + here[dim]
        slots[index] = value
        copies = []
        for n, offset in enumerate(stage_offsets(stage, sizes)):
            copy = pltpu.make_async_remote_copy(
                src_ref=slots.at[index],
                dst_ref=slots.at[index],
                send_sem=send.at[n],
                recv_sem=recv.at[n],
                device_id=at(offset),
                device_id_type=MESH,
            )
            copy.start()
            copies.append(copy)
        return copies

    def stage_sum(slots, copies):
        for copy in copies:
            copy.wait()
        total = slots[0]
        for n in range(1, slots.shape[0]):
            total = total + slots[n]
        return total

    copies_a = stage_start(STAGES[0], slots_a, send_a, recv_a, partial)

    for copy in loads[3 + N_LOADS :]:
        copy.wait()
    for m in range(MODES):
        mine[m : m + 1, :] = jnp.where(live, shape_rows[m], 0.0)
    mine[MODES : MODES + 1, :] = cell[...].astype(F32)
    mine[MODES + 1 :, :] = jnp.zeros((mine.shape[0] - MODES - 1, n_surf), F32)
    surfels = []
    for n, offset in enumerate(wall_offsets(sizes)):
        copy = pltpu.make_async_remote_copy(
            src_ref=mine,
            dst_ref=theirs.at[n],
            send_sem=surf_send.at[n],
            recv_sem=surf_recv.at[n],
            device_id=at(offset),
            device_id_type=MESH,
        )
        copy.start()
        surfels.append(copy)

    def collide(z, packed):
        f = [pops[i, z] for i in range(19)]
        density = dens[z + 1]
        inverse = 1.0 / density
        u = []
        for axis in range(3):
            plus, minus = moving(axis, 1), moving(axis, -1)
            total = f[plus[0]] - f[minus[0]]
            for i, j in zip(plus[1:], minus[1:]):
                total = total + (f[i] - f[j])
            u.append(total * inverse)
        base = 1.0 - 1.5 * (u[0] * u[0] + u[1] * u[1] + u[2] * u[2])
        fixed = solid[z] == 1
        scaled = [OMEGA * w * density for w in WEIGHTS]
        new = [None] * 19
        new[0] = jnp.where(fixed, f[0], (1.0 - OMEGA) * f[0] + scaled[0] * base)
        for i in range(1, 19, 2):
            proj = None
            for axis in range(3):
                comp = VELOCITY[i][axis]
                if comp:
                    term = u[axis] if comp == 1 else -u[axis]
                    proj = term if proj is None else proj + term
            even = scaled[i] * (base + 4.5 * (proj * proj))
            odd = scaled[i] * (3.0 * proj)
            new[i] = jnp.where(fixed, f[i + 1], (1.0 - OMEGA) * f[i] + (even + odd))
            new[i + 1] = jnp.where(fixed, f[i], (1.0 - OMEGA) * f[i + 1] + (even - odd))
        for i in range(19):
            post[PLACE[i], z + 1] = new[i]
        packed = list(packed)
        for a in range(2):
            edge = rows - 1 if a == 0 else 0
            for k, i in enumerate(X_GROUP[a]):
                xs[a, k, z] = new[i][edge : edge + 1]
            xs[a, 5, z] = density[edge : edge + 1]
            edge = width - 1 if a == 0 else 0
            for j, value in enumerate([new[i] for i in Y_GROUP[a]] + [density]):
                column = jnp.broadcast_to(value[:, edge : edge + 1], (rows, width))
                packed[a] = jnp.where(lane == j * depth + z, column, packed[a])
        return tuple(packed)

    zero = jnp.zeros((rows, width), F32)
    packed = lax.fori_loop(0, depth, collide, (zero, zero))
    for a in range(2):
        ys[a] = packed[a]

    halo = []

    def send(src, dst, offset):
        copy = pltpu.make_async_remote_copy(
            src_ref=src,
            dst_ref=dst,
            send_sem=send_sem.at[len(halo)],
            recv_sem=recv_sem.at[len(halo)],
            device_id=at(offset),
            device_id_type=MESH,
        )
        copy.start()
        halo.append(copy)
        return copy

    for a, s in enumerate(SIGNS):
        group = Z_GROUP[a]
        first = a * len(group)
        source, target = (depth, 0) if a == 0 else (1, depth + 1)
        send(xs.at[a], xh.at[a, :, pl.ds(1, depth)], (s, 0, 0))
        send(
            post.at[pl.ds(first, len(group)), source],
            post.at[pl.ds(first, len(group)), target],
            (0, 0, s),
        )
        send(dens.at[source], dens.at[target], (0, 0, s))
        send(ys.at[a], yh.at[a], (0, s, 0))
        for b, t in enumerate(SIGNS):
            send(ys.at[a], yxh.at[a, b], (t, s, 0))
            send(ys.at[a], yzh.at[a, b], (0, s, t))
            k = [i for i in range(5) if VELOCITY[X_GROUP[a][i]][2] == t][0]
            source, target = (depth - 1, 0) if b == 0 else (0, depth + 1)
            send(xs.at[a, k, source], xh.at[a, k, target], (s, 0, t))
            send(xs.at[a, 5, source], xh.at[a, 5, target], (s, 0, t))

    mode_id = lax.broadcasted_iota(jnp.int32, (MODES, PANELS), 0)
    diagonal = lax.broadcasted_iota(jnp.int32, (MODES, MODES), 0) == lax.broadcasted_iota(
        jnp.int32, (MODES, MODES), 1
    )
    factor = jnp.sum(jnp.where(diagonal, compliance[...], 0.0), axis=1, keepdims=True)
    drives = panel_mode[...] == mode_id

    load_a = stage_sum(slots_a, copies_a)
    copies_b = stage_start(STAGES[1], slots_b, send_b, recv_b, load_a)
    def arrived(moved):
        columns = []
        for a in range(2):
            face = yh[a] + y_flux[a] if moved else yh[a]
            result = face
            for j, i in enumerate(Y_GROUP[a]):
                cx, _, cz = VELOCITY[i]
                mine = (lane >= j * depth) & (lane < (j + 1) * depth)
                if cx and moved:
                    b = SIGNS.index(cx)
                    edge = pltpu.roll(yxh[a, b] + yx_flux[a][b], cx % rows, 0)
                    whole = pltpu.roll(face, cx % rows, 0)
                    whole = jnp.where(sub == (0 if cx == 1 else rows - 1), edge, whole)
                    result = jnp.where(mine, whole, result)
                if cz and not moved:
                    b = SIGNS.index(cz)
                    whole = pltpu.roll(face, cz % width, 1)
                    wrapped = pltpu.roll(yzh[a, b], (-cz * (depth - 1)) % width, 1)
                    spot = j * depth if cz == 1 else (j + 1) * depth - 1
                    whole = jnp.where(lane == spot, wrapped, whole)
                    result = jnp.where(mine, whole, result)
            columns.append(result)
        return columns

    def finish(moved, z, columns):
        for i in range(19):
            cx, cy, cz = VELOCITY[i]
            if bool(cx) != moved:
                continue
            source = z + 1 - cz
            value = post[PLACE[i], source]
            if cx:
                a = SIGNS.index(cx)
                k = X_GROUP[a].index(i)
                value = value + COEF[i] * wall[source]
                line = xh[a, k, source] + COEF[i] * wxh[a, source]
                value = pltpu.roll(value, cx % rows, 0)
                value = jnp.where(sub == (0 if cx == 1 else rows - 1), line, value)
            if cy:
                a = SIGNS.index(cy)
                j = Y_GROUP[a].index(i)
                value = pltpu.roll(value, cy % width, 1)
                column = jnp.broadcast_to(
                    columns[a][:, j * depth : j * depth + 1], (rows, width)
                )
                value = jnp.where(lane == (0 if cy == 1 else width - 1), column, value)
            out[i, z] = value
        return tuple(pltpu.roll(c, width - 1, 1) for c in columns)

    for copy in halo:
        copy.wait()
    lax.fori_loop(0, depth, functools.partial(finish, False), tuple(arrived(False)))

    for copy in surfels:
        copy.wait()
    masks = []
    places = wall_offsets(sizes)
    spot = lax.broadcasted_iota(jnp.int32, (width, n_surf), 0)
    spot_z = lax.rem(spot, depth)
    row_id = lax.broadcasted_iota(jnp.int32, (rows, n_surf), 0)
    level_id = lax.broadcasted_iota(jnp.int32, (depth, n_surf), 0)
    for index, (kind, a, b, velocity) in enumerate(WALLS):
        offset = places.index(tuple(c % n for c, n in zip(velocity, sizes)))
        cells_of = theirs[offset, MODES : MODES + 1, :].astype(jnp.int32)
        cy = lax.rem(cells_of, width)
        cx = lax.rem(lax.div(cells_of, width), rows)
        cz = lax.div(cells_of, width * rows)
        picked = (spot_z == cz) if kind[0] == "y" else (spot == cy)
        picks[index] = jnp.where(picked, 1.0, 0.0).astype(BF16)
        if kind == "x":
            mask = (level_id == cz) & (cx == (rows - 1 if a == 0 else 0))
        elif kind[0] == "y":
            mask = (row_id == cx) & (cy == (width - 1 if a == 0 else 0))
        else:
            up = a if kind == "z" else b
            mask = (row_id == cx) & (cz == (depth - 1 if up == 0 else 0))
        masks.append((mask, offset))

    force = stage_sum(slots_b, copies_b)[:, :PANELS]
    force_out[...] = force
    amp = factor * jnp.sum(jnp.where(drives, force, 0.0), axis=1, keepdims=True)
    amp_out[...] = jnp.sum(jnp.where(diagonal, amp, 0.0), axis=0, keepdims=True)

    def speed_of(block):
        return WALL_SCALE * jnp.sum(amp * block[:MODES, :], axis=0, keepdims=True)

    high, low = halves(jnp.where(on_row, speed_of(mine[...]), 0.0))
    flux = dot_nt(high, pick_col) + dot_nt(low, pick_col)
    flux = flux.reshape(depth, rows, width) * dens[pl.ds(1, depth)]
    wall[pl.ds(1, depth)] = flux

    speeds = [speed_of(theirs[n]) for n in range(len(surfels))]

    def spread(index, mask, offset):
        high, low = halves(jnp.where(mask, speeds[offset], 0.0))
        return dot_nt(high, picks[index]) + dot_nt(low, picks[index])

    def on_lanes(a, tile, flux):
        result = jnp.zeros_like(tile)
        for j, i in enumerate(Y_GROUP[a]):
            if VELOCITY[i][0]:
                mine_lanes = (lane >= j * depth) & (lane < (j + 1) * depth)
                moved = pltpu.roll(tile, (j - 5) * depth % width, 1)
                result = jnp.where(mine_lanes, COEF[i] * moved * flux, result)
        return result

    y_flux = [None, None]
    yx_flux = [[None, None], [None, None]]
    for index, (kind, a, b, velocity) in enumerate(WALLS):
        mask, offset = masks[index]
        flux = spread(index, mask, offset)
        if kind == "x":
            for z in range(depth):
                wxh[a, z + 1] = flux[z : z + 1] * xh[a, 5, z + 1]
        elif kind == "z":
            slot = 0 if a == 0 else depth + 1
            wall[slot] = flux * dens[slot]
        elif kind == "xz":
            edge = rows - 1 if a == 0 else 0
            slot = 0 if b == 0 else depth + 1
            wxh[a, slot] = flux[edge : edge + 1] * xh[a, 5, slot]
        elif kind == "y":
            y_flux[a] = on_lanes(a, yh[a], flux)
        else:
            yx_flux[a][b] = on_lanes(a, yxh[a, b], flux)

    columns = arrived(True)
    lax.fori_loop(0, depth, functools.partial(finish, True), tuple(columns))


def per_device(sizes, pops, solid, cell, panel, area, shapes, panel_mode, compliance):
    depth, rows, width = pops.shape[1:]
    n_surf = cell.shape[-1]
    count = {a: n for a, n in zip(AXES, sizes)}
    n_a, n_b = (
        functools.reduce(lambda x, y: x * y, [count[a] for a in stage]) for stage in STAGES
    )
    vmem = pl.BlockSpec(memory_space=pltpu.VMEM)
    tile = (rows, width)
    messages = 18 + 6
    n_wall = len(wall_offsets(sizes))
    dma = pltpu.SemaphoreType.DMA
    read, force, amp = pl.pallas_call(
        functools.partial(kernel, sizes),
        out_shape=(
            jax.ShapeDtypeStruct(pops.shape, F32),
            jax.ShapeDtypeStruct((1, PANELS), F32),
            jax.ShapeDtypeStruct((1, MODES), F32),
        ),
        in_specs=[pl.BlockSpec(memory_space=pltpu.HBM)] * 8,
        out_specs=(vmem,) * 3,
        scratch_shapes=[
            pltpu.VMEM(pops.shape, F32),
            pltpu.VMEM(solid.shape, jnp.int32),
            pltpu.VMEM((1, n_surf), jnp.int32),
            pltpu.VMEM((1, n_surf), jnp.int32),
            pltpu.VMEM((1, n_surf), F32),
            pltpu.VMEM((MODES, 1, n_surf), F32),
            pltpu.VMEM((1, PANELS), jnp.int32),
            pltpu.VMEM((1, MODES), F32),
            pltpu.VMEM((16, n_surf), F32),
            dma((7 + N_LOADS,)),
            pltpu.VMEM((19, depth + 2) + tile, F32),
            pltpu.VMEM((depth + 2,) + tile, F32),
            pltpu.VMEM((depth + 2,) + tile, F32),
            pltpu.VMEM((2, 6, depth, 1, width), F32),
            pltpu.VMEM((2, 6, depth + 2, 1, width), F32),
            pltpu.VMEM((2, depth + 2, 1, width), F32),
            pltpu.VMEM((2,) + tile, F32),
            pltpu.VMEM((2,) + tile, F32),
            pltpu.VMEM((2, 2) + tile, F32),
            pltpu.VMEM((2, 2) + tile, F32),
            pltpu.VMEM((n_wall, 16, n_surf), F32),
            pltpu.VMEM((len(WALLS), width, n_surf), BF16),
            dma((n_wall,)),
            dma((n_wall,)),
            pltpu.VMEM((n_a, 1, width), F32),
            pltpu.VMEM((n_b, 1, width), F32),
            dma((messages,)),
            dma((messages,)),
            dma((n_a - 1,)),
            dma((n_a - 1,)),
            dma((n_b - 1,)),
            dma((n_b - 1,)),
        ],
        compiler_params=pltpu.CompilerParams(
            collective_id=0, has_side_effects=True, vmem_limit_bytes=62 * 1024 * 1024
        ),
    )(
        pops,
        solid,
        cell.reshape(1, n_surf),
        panel.reshape(1, n_surf),
        area.reshape(1, n_surf),
        shapes.reshape(MODES, 1, n_surf),
        panel_mode.reshape(1, PANELS),
        compliance.reshape(1, MODES),
    )
    return read, force.reshape(PANELS), amp.reshape(MODES)


def solution(mesh):
    placed = (
        P(None, "gz", "gx", "gy"),
        P("gz", "gx", "gy"),
        P("gz", "gx", "gy", None),
        P("gz", "gx", "gy", None),
        P("gz", "gx", "gy", None),
        P("gz", "gx", "gy", None, None),
        P(),
        P(),
    )
    return jax.shard_map(
        functools.partial(per_device, tuple(mesh.shape[a] for a in AXES)),
        mesh=mesh,
        in_specs=placed,
        out_specs=(P(None, "gz", "gx", "gy"), P(), P()),
        check_vma=False,
    )
```

```python
import functools

import jax
import jax.numpy as jnp
from jax import lax
from jax.experimental import pallas as pl
from jax.experimental.pallas import tpu as pltpu
from jax.sharding import PartitionSpec as P

PANELS = 40
MODES = 12
VELOCITY = (
    (0, 0, 0),
    (1, 0, 0),
    (-1, 0, 0),
    (0, 1, 0),
    (0, -1, 0),
    (0, 0, 1),
    (0, 0, -1),
    (1, 1, 0),
    (-1, -1, 0),
    (1, -1, 0),
    (-1, 1, 0),
    (1, 0, 1),
    (-1, 0, -1),
    (1, 0, -1),
    (-1, 0, 1),
    (0, 1, 1),
    (0, -1, -1),
    (0, 1, -1),
    (0, -1, 1),
)
WEIGHTS = (1.0 / 3.0,) + (1.0 / 18.0,) * 6 + (1.0 / 36.0,) * 12
OMEGA = 1.0 / 0.6
WALL_SCALE = 0.02
COEF = tuple(6.0 * w * v[0] for w, v in zip(WEIGHTS, VELOCITY))
SIGNS = (1, -1)


def moving(axis, sign):
    return tuple(i for i in range(19) if VELOCITY[i][axis] == sign)


X_GROUP = tuple(moving(0, s) for s in SIGNS)
Y_GROUP = tuple(moving(1, s) for s in SIGNS)
Z_GROUP = tuple(moving(2, s) for s in SIGNS)
ORDER = Z_GROUP[0] + Z_GROUP[1] + tuple(i for i in range(19) if VELOCITY[i][2] == 0)
PLACE = tuple(ORDER.index(i) for i in range(19))
AXES = ("gx", "gy", "gz")
STAGES = (("gx",), ("gy", "gz"))
MESH = pl.DeviceIdType.MESH
N_LOADS = 4
F32 = jnp.float32
BF16 = jnp.bfloat16


def halves(x):
    high = x.astype(BF16)
    return high, (x - high.astype(F32)).astype(BF16)


def dot(a, b):
    return jnp.dot(a, b, preferred_element_type=F32)


def dot_nt(a, b):
    return lax.dot_general(a, b, (((1,), (1,)), ((), ())), preferred_element_type=F32)


def shift_of(velocity):
    return (velocity[0], velocity[1], velocity[2])


def offsets_of(sizes):
    found = []
    for i in range(1, 19):
        found.append(tuple(c % n for c, n in zip(VELOCITY[i], sizes)))
    for stage in STAGES:
        for offset in stage_offsets(stage, sizes):
            found.append(offset)
    return sorted(set(found))


def stage_offsets(stage, sizes):
    result = [(0, 0, 0)]
    for dim, axis in enumerate(AXES):
        if axis in stage:
            result = [
                tuple(k if d == dim else o[d] for d in range(3))
                for o in result
                for k in range(sizes[dim])
            ]
    return [o for o in result if o != (0, 0, 0)]


WALLS = []
for first, s in enumerate(SIGNS):
    WALLS.append(("x", first, 0, (s, 0, 0)))
    WALLS.append(("y", first, 0, (0, s, 0)))
    WALLS.append(("z", first, 0, (0, 0, s)))
    for second, t in enumerate(SIGNS):
        WALLS.append(("xz", first, second, (s, 0, t)))
        WALLS.append(("yx", first, second, (t, s, 0)))


def wall_offsets(sizes):
    return sorted({tuple(c % n for c, n in zip(w[3], sizes)) for w in WALLS})


def kernel(
    sizes,
    pops_in,
    solid_in,
    cell_in,
    panel_in,
    area_in,
    shapes_in,
    panel_mode_in,
    compliance_in,
    out,
    force_out,
    amp_out,
    pops,
    solid,
    cell,
    panel,
    area,
    shape_rows,
    panel_mode,
    compliance,
    mine,
    load_sem,
    post,
    dens,
    wall,
    xs,
    xh,
    wxh,
    ys,
    yh,
    yxh,
    yzh,
    theirs,
    picks,
    surf_send,
    surf_recv,
    slots_a,
    slots_b,
    send_sem,
    recv_sem,
    send_a,
    recv_a,
    send_b,
    recv_b,
):
    depth, rows, width = pops.shape[1:]
    cells = depth * rows
    here = tuple(lax.axis_index(a) for a in AXES)

    def at(offset):
        return tuple(lax.rem(h + o % n, n) if o % n else h for h, o, n in zip(here, offset, sizes))

    partners = offsets_of(sizes)
    barrier = pltpu.get_barrier_semaphore()
    for offset in partners:
        pl.semaphore_signal(barrier, inc=1, device_id=at(offset), device_id_type=MESH)

    pairs = [(cell_in, cell), (panel_in, panel), (area_in, area)]
    pairs += [(solid_in, solid), (shapes_in, shape_rows)]
    pairs += [(panel_mode_in, panel_mode), (compliance_in, compliance)]
    part = depth // N_LOADS
    cuts = [pl.ds(n * part, part) for n in range(N_LOADS)]
    pairs = pairs[:3] + [(pops_in.at[:, c], pops.at[:, c]) for c in cuts] + pairs[3:]
    loads = []
    for n, (src, dst) in enumerate(pairs):
        loads.append(pltpu.make_async_copy(src, dst, load_sem.at[n]))
        loads[n].start()

    lane = lax.broadcasted_iota(jnp.int32, (rows, width), 1)
    sub = lax.broadcasted_iota(jnp.int32, (rows, width), 0)

    for copy in loads[:3]:
        copy.wait()
    live = panel[...] >= 0
    col = lax.rem(cell[...], width)
    row = lax.div(cell[...], width)
    n_surf = cell.shape[1]
    pick_col = jnp.where(
        lax.broadcasted_iota(jnp.int32, (width, n_surf), 0) == col, 1.0, 0.0
    ).astype(BF16)
    on_row = lax.broadcasted_iota(jnp.int32, (cells, n_surf), 0) == row

    def add_up(z, carry):
        density = pops[0, z]
        for i in range(1, 19):
            density = density + pops[i, z]
        dens[z + 1] = density
        return carry

    for n in range(N_LOADS):
        loads[3 + n].wait()
        lax.fori_loop(n * part, (n + 1) * part, add_up, 0, unroll=True)
    gauge_high, gauge_low = halves(dens[pl.ds(1, depth)].reshape(cells, width) - 1.0)
    by_row = dot(gauge_high, pick_col) + dot(gauge_low, pick_col)
    excess = jnp.sum(jnp.where(on_row, by_row, 0.0), axis=0, keepdims=True)
    contrib = jnp.where(live, area[...] * (excess / 3.0), 0.0)
    pick_panel = jnp.where(
        lax.broadcasted_iota(jnp.int32, (width, n_surf), 0) == panel[...], 1.0, 0.0
    ).astype(BF16)
    contrib_high, contrib_low = halves(jnp.broadcast_to(contrib, (8, n_surf)))
    partial = dot_nt(contrib_high, pick_panel) + dot_nt(contrib_low, pick_panel)
    partial = partial[0:1]

    pl.semaphore_wait(barrier, len(partners))

    def stage_start(stage, slots, send, recv, value):
        index = 0
        for dim, axis in enumerate(AXES):
            if axis in stage:
                index = index * sizes[dim] + here[dim]
        slots[index] = value
        copies = []
        for n, offset in enumerate(stage_offsets(stage, sizes)):
            copy = pltpu.make_async_remote_copy(
                src_ref=slots.at[index],
                dst_ref=slots.at[index],
                send_sem=send.at[n],
                recv_sem=recv.at[n],
                device_id=at(offset),
                device_id_type=MESH,
            )
            copy.start()
            copies.append(copy)
        return copies

    def stage_sum(slots, copies):
        for copy in copies:
            copy.wait()
        total = slots[0]
        for n in range(1, slots.shape[0]):
            total = total + slots[n]
        return total

    copies_a = stage_start(STAGES[0], slots_a, send_a, recv_a, partial)

    for copy in loads[3 + N_LOADS :]:
        copy.wait()
    for m in range(MODES):
        mine[m : m + 1, :] = jnp.where(live, shape_rows[m], 0.0)
    mine[MODES : MODES + 1, :] = cell[...].astype(F32)
    mine[MODES + 1 :, :] = jnp.zeros((mine.shape[0] - MODES - 1, n_surf), F32)
    surfels = []
    for n, offset in enumerate(wall_offsets(sizes)):
        copy = pltpu.make_async_remote_copy(
            src_ref=mine,
            dst_ref=theirs.at[n],
            send_sem=surf_send.at[n],
            recv_sem=surf_recv.at[n],
            device_id=at(offset),
            device_id_type=MESH,
        )
        copy.start()
        surfels.append(copy)

    def collide(z, packed):
        f = [pops[i, z] for i in range(19)]
        density = dens[z + 1]
        inverse = 1.0 / density
        u = []
        for axis in range(3):
            plus, minus = moving(axis, 1), moving(axis, -1)
            total = f[plus[0]] - f[minus[0]]
            for i, j in zip(plus[1:], minus[1:]):
                total = total + (f[i] - f[j])
            u.append(total * inverse)
        base = 1.0 - 1.5 * (u[0] * u[0] + u[1] * u[1] + u[2] * u[2])
        fixed = solid[z] == 1
        scaled = [OMEGA * w * density for w in WEIGHTS]
        new = [None] * 19
        new[0] = jnp.where(fixed, f[0], (1.0 - OMEGA) * f[0] + scaled[0] * base)
        for i in range(1, 19, 2):
            proj = None
            for axis in range(3):
                comp = VELOCITY[i][axis]
                if comp:
                    term = u[axis] if comp == 1 else -u[axis]
                    proj = term if proj is None else proj + term
            even = scaled[i] * (base + 4.5 * (proj * proj))
            odd = scaled[i] * (3.0 * proj)
            new[i] = jnp.where(fixed, f[i + 1], (1.0 - OMEGA) * f[i] + (even + odd))
            new[i + 1] = jnp.where(fixed, f[i], (1.0 - OMEGA) * f[i + 1] + (even - odd))
        for i in range(19):
            post[PLACE[i], z + 1] = new[i]
        packed = list(packed)
        for a in range(2):
            edge = rows - 1 if a == 0 else 0
            for k, i in enumerate(X_GROUP[a]):
                xs[a, k, z] = new[i][edge : edge + 1]
            xs[a, 5, z] = density[edge : edge + 1]
            edge = width - 1 if a == 0 else 0
            for j, value in enumerate([new[i] for i in Y_GROUP[a]] + [density]):
                column = jnp.broadcast_to(value[:, edge : edge + 1], (rows, width))
                packed[a] = jnp.where(lane == j * depth + z, column, packed[a])
        return tuple(packed)

    zero = jnp.zeros((rows, width), F32)
    packed = lax.fori_loop(0, depth, collide, (zero, zero))
    for a in range(2):
        ys[a] = packed[a]

    halo = []

    def send(src, dst, offset):
        copy = pltpu.make_async_remote_copy(
            src_ref=src,
            dst_ref=dst,
            send_sem=send_sem.at[len(halo)],
            recv_sem=recv_sem.at[len(halo)],
            device_id=at(offset),
            device_id_type=MESH,
        )
        copy.start()
        halo.append(copy)
        return copy

    for a, s in enumerate(SIGNS):
        group = Z_GROUP[a]
        first = a * len(group)
        source, target = (depth, 0) if a == 0 else (1, depth + 1)
        send(xs.at[a], xh.at[a, :, pl.ds(1, depth)], (s, 0, 0))
        send(
            post.at[pl.ds(first, len(group)), source],
            post.at[pl.ds(first, len(group)), target],
            (0, 0, s),
        )
        send(dens.at[source], dens.at[target], (0, 0, s))
        send(ys.at[a], yh.at[a], (0, s, 0))
        for b, t in enumerate(SIGNS):
            send(ys.at[a], yxh.at[a, b], (t, s, 0))
            send(ys.at[a], yzh.at[a, b], (0, s, t))
            k = [i for i in range(5) if VELOCITY[X_GROUP[a][i]][2] == t][0]
            source, target = (depth - 1, 0) if b == 0 else (0, depth + 1)
            send(xs.at[a, k, source], xh.at[a, k, target], (s, 0, t))
            send(xs.at[a, 5, source], xh.at[a, 5, target], (s, 0, t))

    mode_id = lax.broadcasted_iota(jnp.int32, (MODES, PANELS), 0)
    diagonal = lax.broadcasted_iota(jnp.int32, (MODES, MODES), 0) == lax.broadcasted_iota(
        jnp.int32, (MODES, MODES), 1
    )
    factor = jnp.sum(jnp.where(diagonal, compliance[...], 0.0), axis=1, keepdims=True)
    drives = panel_mode[...] == mode_id

    load_a = stage_sum(slots_a, copies_a)
    copies_b = stage_start(STAGES[1], slots_b, send_b, recv_b, load_a)
    def arrived(moved):
        columns = []
        for a in range(2):
            face = yh[a] + y_flux[a] if moved else yh[a]
            result = face
            for j, i in enumerate(Y_GROUP[a]):
                cx, _, cz = VELOCITY[i]
                mine = (lane >= j * depth) & (lane < (j + 1) * depth)
                if cx and moved:
                    b = SIGNS.index(cx)
                    edge = pltpu.roll(yxh[a, b] + yx_flux[a][b], cx % rows, 0)
                    whole = pltpu.roll(face, cx % rows, 0)
                    whole = jnp.where(sub == (0 if cx == 1 else rows - 1), edge, whole)
                    result = jnp.where(mine, whole, result)
                if cz and not moved:
                    b = SIGNS.index(cz)
                    whole = pltpu.roll(face, cz % width, 1)
                    wrapped = pltpu.roll(yzh[a, b], (-cz * (depth - 1)) % width, 1)
                    spot = j * depth if cz == 1 else (j + 1) * depth - 1
                    whole = jnp.where(lane == spot, wrapped, whole)
                    result = jnp.where(mine, whole, result)
            columns.append(result)
        return columns

    def finish(moved, z, columns):
        for i in range(19):
            cx, cy, cz = VELOCITY[i]
            if bool(cx) != moved:
                continue
            source = z + 1 - cz
            value = post[PLACE[i], source]
            if cx:
                a = SIGNS.index(cx)
                k = X_GROUP[a].index(i)
                value = value + COEF[i] * wall[source]
                line = xh[a, k, source] + COEF[i] * wxh[a, source]
                value = pltpu.roll(value, cx % rows, 0)
                value = jnp.where(sub == (0 if cx == 1 else rows - 1), line, value)
            if cy:
                a = SIGNS.index(cy)
                j = Y_GROUP[a].index(i)
                value = pltpu.roll(value, cy % width, 1)
                column = jnp.broadcast_to(
                    columns[a][:, j * depth : j * depth + 1], (rows, width)
                )
                value = jnp.where(lane == (0 if cy == 1 else width - 1), column, value)
            out[i, z] = value
        return tuple(pltpu.roll(c, width - 1, 1) for c in columns)

    for copy in halo:
        copy.wait()
    lax.fori_loop(0, depth, functools.partial(finish, False), tuple(arrived(False)))

    for copy in surfels:
        copy.wait()
    masks = []
    places = wall_offsets(sizes)
    spot = lax.broadcasted_iota(jnp.int32, (width, n_surf), 0)
    spot_z = lax.rem(spot, depth)
    row_id = lax.broadcasted_iota(jnp.int32, (rows, n_surf), 0)
    level_id = lax.broadcasted_iota(jnp.int32, (depth, n_surf), 0)
    for index, (kind, a, b, velocity) in enumerate(WALLS):
        offset = places.index(tuple(c % n for c, n in zip(velocity, sizes)))
        cells_of = theirs[offset, MODES : MODES + 1, :].astype(jnp.int32)
        cy = lax.rem(cells_of, width)
        cx = lax.rem(lax.div(cells_of, width), rows)
        cz = lax.div(cells_of, width * rows)
        picked = (spot_z == cz) if kind[0] == "y" else (spot == cy)
        picks[index] = jnp.where(picked, 1.0, 0.0).astype(BF16)
        if kind == "x":
            mask = (level_id == cz) & (cx == (rows - 1 if a == 0 else 0))
        elif kind[0] == "y":
            mask = (row_id == cx) & (cy == (width - 1 if a == 0 else 0))
        else:
            up = a if kind == "z" else b
            mask = (row_id == cx) & (cz == (depth - 1 if up == 0 else 0))
        masks.append((mask, offset))

    force = stage_sum(slots_b, copies_b)[:, :PANELS]
    force_out[...] = force
    amp = factor * jnp.sum(jnp.where(drives, force, 0.0), axis=1, keepdims=True)
    amp_out[...] = jnp.sum(jnp.where(diagonal, amp, 0.0), axis=0, keepdims=True)

    def speed_of(block):
        return WALL_SCALE * jnp.sum(amp * block[:MODES, :], axis=0, keepdims=True)

    high, low = halves(jnp.where(on_row, speed_of(mine[...]), 0.0))
    flux = dot_nt(high, pick_col) + dot_nt(low, pick_col)
    flux = flux.reshape(depth, rows, width) * dens[pl.ds(1, depth)]
    wall[pl.ds(1, depth)] = flux

    speeds = [speed_of(theirs[n]) for n in range(len(surfels))]

    def spread(index, mask, offset):
        high, low = halves(jnp.where(mask, speeds[offset], 0.0))
        return dot_nt(high, picks[index]) + dot_nt(low, picks[index])

    def on_lanes(a, tile, flux):
        result = jnp.zeros_like(tile)
        for j, i in enumerate(Y_GROUP[a]):
            if VELOCITY[i][0]:
                mine_lanes = (lane >= j * depth) & (lane < (j + 1) * depth)
                moved = pltpu.roll(tile, (j - 5) * depth % width, 1)
                result = jnp.where(mine_lanes, COEF[i] * moved * flux, result)
        return result

    y_flux = [None, None]
    yx_flux = [[None, None], [None, None]]
    for index, (kind, a, b, velocity) in enumerate(WALLS):
        mask, offset = masks[index]
        flux = spread(index, mask, offset)
        if kind == "x":
            for z in range(depth):
                wxh[a, z + 1] = flux[z : z + 1] * xh[a, 5, z + 1]
        elif kind == "z":
            slot = 0 if a == 0 else depth + 1
            wall[slot] = flux * dens[slot]
        elif kind == "xz":
            edge = rows - 1 if a == 0 else 0
            slot = 0 if b == 0 else depth + 1
            wxh[a, slot] = flux[edge : edge + 1] * xh[a, 5, slot]
        elif kind == "y":
            y_flux[a] = on_lanes(a, yh[a], flux)
        else:
            yx_flux[a][b] = on_lanes(a, yxh[a, b], flux)

    columns = arrived(True)
    lax.fori_loop(0, depth, functools.partial(finish, True), tuple(columns), unroll=2)


def per_device(sizes, pops, solid, cell, panel, area, shapes, panel_mode, compliance):
    depth, rows, width = pops.shape[1:]
    n_surf = cell.shape[-1]
    count = {a: n for a, n in zip(AXES, sizes)}
    n_a, n_b = (
        functools.reduce(lambda x, y: x * y, [count[a] for a in stage]) for stage in STAGES
    )
    vmem = pl.BlockSpec(memory_space=pltpu.VMEM)
    tile = (rows, width)
    messages = 18 + 6
    n_wall = len(wall_offsets(sizes))
    dma = pltpu.SemaphoreType.DMA
    read, force, amp = pl.pallas_call(
        functools.partial(kernel, sizes),
        out_shape=(
            jax.ShapeDtypeStruct(pops.shape, F32),
            jax.ShapeDtypeStruct((1, PANELS), F32),
            jax.ShapeDtypeStruct((1, MODES), F32),
        ),
        in_specs=[pl.BlockSpec(memory_space=pltpu.HBM)] * 8,
        out_specs=(vmem,) * 3,
        scratch_shapes=[
            pltpu.VMEM(pops.shape, F32),
            pltpu.VMEM(solid.shape, jnp.int32),
            pltpu.VMEM((1, n_surf), jnp.int32),
            pltpu.VMEM((1, n_surf), jnp.int32),
            pltpu.VMEM((1, n_surf), F32),
            pltpu.VMEM((MODES, 1, n_surf), F32),
            pltpu.VMEM((1, PANELS), jnp.int32),
            pltpu.VMEM((1, MODES), F32),
            pltpu.VMEM((16, n_surf), F32),
            dma((7 + N_LOADS,)),
            pltpu.VMEM((19, depth + 2) + tile, F32),
            pltpu.VMEM((depth + 2,) + tile, F32),
            pltpu.VMEM((depth + 2,) + tile, F32),
            pltpu.VMEM((2, 6, depth, 1, width), F32),
            pltpu.VMEM((2, 6, depth + 2, 1, width), F32),
            pltpu.VMEM((2, depth + 2, 1, width), F32),
            pltpu.VMEM((2,) + tile, F32),
            pltpu.VMEM((2,) + tile, F32),
            pltpu.VMEM((2, 2) + tile, F32),
            pltpu.VMEM((2, 2) + tile, F32),
            pltpu.VMEM((n_wall, 16, n_surf), F32),
            pltpu.VMEM((len(WALLS), width, n_surf), BF16),
            dma((n_wall,)),
            dma((n_wall,)),
            pltpu.VMEM((n_a, 1, width), F32),
            pltpu.VMEM((n_b, 1, width), F32),
            dma((messages,)),
            dma((messages,)),
            dma((n_a - 1,)),
            dma((n_a - 1,)),
            dma((n_b - 1,)),
            dma((n_b - 1,)),
        ],
        compiler_params=pltpu.CompilerParams(
            collective_id=0, has_side_effects=True, vmem_limit_bytes=32 * 1024 * 1024
        ),
    )(
        *(
            pltpu.with_memory_space_constraint(x, pltpu.HBM)
            for x in (
                pops,
                solid,
                cell.reshape(1, n_surf),
                panel.reshape(1, n_surf),
                area.reshape(1, n_surf),
                shapes.reshape(MODES, 1, n_surf),
                panel_mode.reshape(1, PANELS),
                compliance.reshape(1, MODES),
            )
        )
    )
    return read, force.reshape(PANELS), amp.reshape(MODES)


def solution(mesh):
    placed = (
        P(None, "gz", "gx", "gy"),
        P("gz", "gx", "gy"),
        P("gz", "gx", "gy", None),
        P("gz", "gx", "gy", None),
        P("gz", "gx", "gy", None),
        P("gz", "gx", "gy", None, None),
        P(),
        P(),
    )
    return jax.shard_map(
        functools.partial(per_device, tuple(mesh.shape[a] for a in AXES)),
        mesh=mesh,
        in_specs=placed,
        out_specs=(P(None, "gz", "gx", "gy"), P(), P()),
        check_vma=False,
    )
```
